32 devices in a mesh: gx: 8 (over z, x), gy: 4 (over y, core).
Axes of the slice: x: 2, y: 2, z: 4, core: 2. Of those that a mesh axis runs over, the one named last changes fastest.
Arguments:
- amplitudes: float32 [2, 512, 128, 512], P(None, 'gx', None, 'gy'), may hold values from -6 to 6
- integrals: float32 [2, 32, 128, 128, 512], P(None, 'gy', None, 'gx'), may hold values from -0.046875 to 0.046875
- virt_count: int32 [8], replicated, may hold values from 24 to 128, as said below
- pair_irrep: int32 [8], replicated, may hold values from 0 to 7, as said below
- slab_index: int32 [1], replicated, may hold values from 0 to 15
- occ_energy: float32 [64], replicated, may hold values from -2 to -0.3
- virt_energy: float32 [512], replicated, may hold values from 0.1 to 3
Outputs:
- update: float32 [2, 512, 32, 128], P(None, 'gx', 'gy')
The draws below stay inside these ranges and needn't reach their ends.
Inputs may be any that keep to these rules, and one draw needn't show every extreme that they name: `virt_count`: entry k counts the virtual orbitals of irrep k; they sum to 512 and the largest is exactly 128. `pair_irrep`: a permutation of the irreps.
All inputs are finite; a program needn't handle non-finite values.
Results may differ from the reference program's by a relative error of at most 0.0001.
Values sent between devices are 32-bit elements; how exact they have to be, the bound alone decides.
A program may use at most 192 MiB of HBM per device.

```python
import jax
import jax.numpy as jnp
from jax import lax

OCC = 64
VIRT = 512
SLAB = 32
IRREPS = 8
SYMS = 2
MAXIRR = 128
IJP = 512


def draw_virt_count(key, part):
    orbital_unit = VIRT // 64
    first_key, second_key = jax.random.split(jax.random.fold_in(key, 11))
    pair_low = jax.random.randint(first_key, (3,), 3 * orbital_unit, 10 * orbital_unit + 1).astype(jnp.int32)
    counts_list = jnp.concatenate([jnp.array([16 * orbital_unit, 9 * orbital_unit], jnp.int32), pair_low, (13 * orbital_unit - pair_low).astype(jnp.int32)])
    shuffle = jax.random.permutation(second_key, IRREPS)
    return counts_list[shuffle].astype(jnp.int32)


def draw_pair_irrep(key, part):
    shuffle = jax.random.permutation(jax.random.fold_in(key, 23), IRREPS)
    return shuffle.astype(jnp.int32)


def with_spikes(values, own_key, source, target, blocks, factor):
    owner, partner = [(jnp.arange(values.shape[position]) // (values.shape[position] // blocks)).reshape([-1 if axis == position else 1 for axis in range(values.ndim)]) for position in (source, target)]
    chosen = jax.random.permutation(own_key, blocks)[partner]
    strong = (owner == chosen) | (owner == (partner + blocks // 2) % blocks)
    return jnp.where(strong, factor * values, values)


def block_scale(rng, shape, pieces, least, largest):
    def one(dim, shards_of):
        heights = jax.random.uniform(jax.random.fold_in(jax.random.fold_in(rng, 6), dim), (shards_of,), jnp.float32, least / len(pieces), largest / len(pieces))
        return jnp.repeat(jnp.exp(heights), shape[dim] // shards_of).reshape((-1,) + (1,) * (len(shape) - dim - 1))

    level = one(*pieces[0])
    for cut in pieces[1:]:
        level = level * one(*cut)
    return level


def scatter_about(own_key, shape, deviation, most, cuts=(), held_as=jnp.bfloat16):
    values = deviation * jax.random.normal(own_key, shape, jnp.float32)
    if cuts:
        values = values * block_scale(own_key, shape, cuts, -0.22, 0.18)
    return jnp.clip(values, -most, most).astype(held_as)


def noise_with(key, extent, scale, most, shards, heavy, kind=jnp.bfloat16):
    values = scale * jax.random.normal(key, extent, jnp.float32)
    if shards:
        values = values * block_scale(key, extent, shards, -0.22, 0.18)
    return jnp.clip(with_spikes(values, jax.random.fold_in(key, 3), *heavy), -most, most).astype(kind)


def setup_inputs(seed: int = 0) -> dict:
    arg_keys = jax.random.split(jax.random.key(seed), 8)
    return {
        "amplitudes": scatter_about(arg_keys[0], (SYMS, IJP, MAXIRR, VIRT), 1.0, 6.0, ((1, 8), (3, 4)), jnp.float32),
        "integrals": noise_with(arg_keys[1], (SYMS, SLAB, MAXIRR, MAXIRR, VIRT), (VIRT * MAXIRR // 2) ** -0.5, 0.046875, ((1, 4), (3, 8)), (3, 2, 8, 2.0), jnp.float32),
        "virt_count": draw_virt_count(jax.random.fold_in(arg_keys[7], 71), 0),
        "pair_irrep": draw_pair_irrep(jax.random.fold_in(arg_keys[7], 71), 0),
        "slab_index": jax.random.randint(arg_keys[4], (1,), 0, VIRT // SLAB).astype(jnp.int32),
        "occ_energy": jnp.clip(jax.random.uniform(arg_keys[5], (OCC,), jnp.float32, -2.0, -0.3), -2.0, -0.3),
        "virt_energy": jnp.clip(jax.random.uniform(arg_keys[6], (VIRT,), jnp.float32, 0.1, 3.0), 0.1, 3.0),
    }


def irrep_of(positions, starts):
    return jnp.sum((positions[..., None] >= starts[1:]).astype(jnp.int32), axis=-1).astype(jnp.int32)


def lookup(entries, positions):
    picks = (positions[..., None] == jnp.arange(IRREPS, dtype=jnp.int32)).astype(entries.dtype)
    return jnp.sum(entries * picks, axis=-1)


def denominator_update(ladder, pair_rows, slab_rows, symmetry, slab_first, starts, virt_count, occ_energy, virt_energy):
    per_irrep = OCC // IRREPS
    occ_irrep = pair_rows // (per_irrep * per_irrep)
    first_occ = per_irrep * occ_irrep + (pair_rows % (per_irrep * per_irrep)) // per_irrep
    second_occ = per_irrep * jnp.bitwise_xor(occ_irrep, symmetry) + pair_rows % per_irrep
    occ_sum = jnp.take(occ_energy, first_occ) + jnp.take(occ_energy, second_occ)
    slab_virt = (SLAB * slab_first + slab_rows).astype(jnp.int32)
    partner = jnp.bitwise_xor(irrep_of(slab_virt, starts), symmetry)
    block_start = lookup(starts, partner)
    block_count = lookup(virt_count, partner)
    slot_range = jnp.arange(MAXIRR, dtype=jnp.int32)
    partner_orbital = jnp.clip(block_start[:, None] + slot_range[None, :], 0, VIRT - 1).astype(jnp.int32)
    slot_valid = slot_range[None, :] < block_count[:, None]
    denominator = occ_sum[:, None, None] - jnp.take(virt_energy, slab_virt)[None, :, None] - jnp.take(virt_energy, partner_orbital)[None]
    return jnp.where(slot_valid[None], ladder / denominator, jnp.zeros_like(ladder))


def reference(amplitudes, integrals, virt_count, pair_irrep, slab_index, occ_energy, virt_energy):
    starts = (jnp.cumsum(virt_count) - virt_count).astype(jnp.int32)
    slot_ids = jnp.arange(MAXIRR, dtype=jnp.int32)
    virt_ids = jnp.arange(VIRT, dtype=jnp.int32)
    base_irrep = irrep_of(virt_ids, starts)
    pair_rows = jnp.arange(IJP, dtype=jnp.int32)
    slab_rows = jnp.arange(SLAB, dtype=jnp.int32)
    updates = []
    for member in range(SYMS):
        symmetry = pair_irrep[member]
        partner = jnp.bitwise_xor(base_irrep, symmetry)
        slot_mask = slot_ids[:, None] < lookup(virt_count, partner)[None, :]
        masked = jnp.where(slot_mask[None], amplitudes[member], jnp.zeros_like(amplitudes[member]))
        ladder = lax.dot_general(masked.reshape(IJP, MAXIRR * VIRT), integrals[member].reshape(SLAB * MAXIRR, MAXIRR * VIRT), (((1,), (1,)), ((), ())), precision=lax.Precision.HIGHEST, preferred_element_type=jnp.float32)
        ladder = ladder.reshape(IJP, SLAB, MAXIRR)
        updates.append(denominator_update(ladder, pair_rows, slab_rows, symmetry, slab_index[0], starts, virt_count, occ_energy, virt_energy))
    return jnp.stack(updates)
```

```python
import jax
import jax.numpy as jnp
from jax import lax
from jax.sharding import PartitionSpec as P

OCC = 64
VIRT = 512
SLAB = 32
IRREPS = 8
SYMS = 2
MAXIRR = 128
PARTS = 2


def irrep_of(positions, starts):
    return jnp.sum((positions[..., None] >= starts[1:]).astype(jnp.int32), axis=-1)


def lookup(entries, positions):
    picks = (positions[..., None] == jnp.arange(IRREPS, dtype=jnp.int32)).astype(entries.dtype)
    return jnp.sum(entries * picks, axis=-1)


def select_entries(entries, positions):
    picks = positions[..., None] == jnp.arange(entries.shape[0], dtype=jnp.int32)
    return jnp.sum(jnp.where(picks, entries, jnp.zeros_like(entries)), axis=-1)


def denominators(
    pair_rows, slab_rows, symmetry, slab_first, starts, virt_count, occ_energy, virt_energy
):
    per_irrep = OCC // IRREPS
    occ_irrep = pair_rows // (per_irrep * per_irrep)
    first_occ = per_irrep * occ_irrep + pair_rows % (per_irrep * per_irrep) // per_irrep
    second_occ = per_irrep * jnp.bitwise_xor(occ_irrep, symmetry) + pair_rows % per_irrep
    occ_sum = select_entries(occ_energy, first_occ) + select_entries(occ_energy, second_occ)
    slab_virt = SLAB * slab_first + slab_rows
    partner = jnp.bitwise_xor(irrep_of(slab_virt, starts), symmetry)
    block_start = lookup(starts, partner)
    block_count = lookup(virt_count, partner)
    slot_range = jnp.arange(MAXIRR, dtype=jnp.int32)
    partner_orbital = jnp.clip(block_start[:, None] + slot_range[None, :], 0, VIRT - 1)
    slot_valid = slot_range[None, :] < block_count[:, None]
    virt_first = select_entries(virt_energy, slab_virt)
    virt_second = select_entries(virt_energy, partner_orbital)
    return occ_sum, virt_first, virt_second, slot_valid


def on_device(amplitudes, integrals, virt_count, pair_irrep, slab_index, occ_energy, virt_energy):
    starts = jnp.cumsum(virt_count) - virt_count
    handled = pair_irrep[:SYMS]
    pair_block = lax.axis_index("gx")
    virt_block = lax.axis_index("gy")
    rows = amplitudes.shape[1]
    width = amplitudes.shape[3]
    slab = integrals.shape[1]
    slot_width = integrals.shape[3]
    part = rows // PARTS
    slot_ids = pair_block * slot_width + jnp.arange(slot_width, dtype=jnp.int32)
    virt_ids = virt_block * width + jnp.arange(width, dtype=jnp.int32)
    partner = jnp.bitwise_xor(irrep_of(virt_ids, starts)[None, :], handled[:, None])
    valid = slot_ids[None, :, None] < lookup(virt_count, partner)[:, None, :]
    pair_rows = pair_block * rows + jnp.arange(rows, dtype=jnp.int32)
    slab_rows = virt_block * slab + jnp.arange(slab, dtype=jnp.int32)
    energies = [
        denominators(
            pair_rows, slab_rows, handled[g], slab_index[0], starts, virt_count, occ_energy, virt_energy
        )
        for g in range(SYMS)
    ]
    updates, sent, masked = [], [], None
    for g in range(SYMS):
        for c in range(PARTS):
            mine = slice(c * part, (c + 1) * part)
            block = amplitudes[g, mine]
            if masked is not None:
                block, masked = lax.optimization_barrier((block, masked))
                sent.append(masked)
            exchanged = lax.all_to_all(block, "gx", split_axis=1, concat_axis=0, tiled=True)
            masked = jnp.where(valid[g][None], exchanged, jnp.zeros_like(exchanged))
    sent.append(masked)
    for g in range(SYMS):
        occ_sum, virt_first, virt_second, slot_valid = energies[g]
        for c in range(PARTS):
            mine = slice(c * part, (c + 1) * part)
            gathered = lax.all_gather(sent[g * PARTS + c], "gy", axis=2, tiled=True)
            ladder = lax.dot_general(
                gathered,
                integrals[g],
                (((1, 2), (2, 3)), ((), ())),
                precision=lax.Precision.HIGH,
                preferred_element_type=jnp.float32,
            )
            reduced = lax.psum_scatter(ladder, "gx", scatter_dimension=0, tiled=True)
            denominator = (
                occ_sum[mine, None, None] - virt_first[None, :, None] - virt_second[None]
            )
            updates.append(
                jnp.where(slot_valid[None], reduced / denominator, jnp.zeros_like(reduced))
            )
    return jnp.concatenate(updates).reshape(SYMS, rows, slab, MAXIRR)


def solution(mesh):
    placed = (P(None, "gx", None, "gy"), P(None, "gy", None, "gx", None), P(), P(), P(), P(), P())
    return jax.shard_map(
        on_device, mesh=mesh, in_specs=placed, out_specs=P(None, "gx", "gy", None), check_vma=False
    )
```
